256 devices in a mesh: dp: 32 (over z, y_hi, core), node: 8 (over x, y_lo).
Axes of the slice: x: 4, y: 4 (y_hi: 2, y_lo: 2; y = y_hi * 2 + y_lo), z: 8, core: 2. Of those that a mesh axis runs over, the one named last changes fastest.
Arguments:
- tokens: bfloat16 [65536, 8192], P(('dp', 'node')), may hold values from -12 to 12
- weight: bfloat16 [8192, 512], P(('dp', 'node')), may hold values from -0.0625 to 0.0625
- cotangent: bfloat16 [65536, 512], P(('dp', 'node')), may hold values from -24 to 24
- amax_history: float32 [3, 16], replicated, may hold values from 0.5 to 8
Outputs:
- keys: bfloat16 [65536, 512], P(('dp', 'node'))
- input_grad: bfloat16 [65536, 8192], P(('dp', 'node'))
- weight_grad: bfloat16 [8192, 512], P(('dp', 'node'))
- new_history: float32 [3, 16], replicated
The draws below stay inside these ranges and needn't reach their ends.
All inputs are finite; a program needn't handle non-finite values.
Results may differ from the reference program's by a relative error of at most 0.0014.
Values may be sent and summed in bfloat16 or wider, within the bound.
No kernel may reach another device: no remote copies, remote signals or barrier semaphores. Data moves between devices by JAX's collectives and lax.ppermute only.
A program may use at most 128 MiB of HBM per device.

```python
import math
import jax
import jax.numpy as jnp
from jax import lax

D = 8192
HIST = 16
KV_WIDTH = 512
TOKENS = 65536


def rising_rows(key, base, lift):
    rows = base.shape[0]
    ramp = 1.0 + 2.0 * jnp.arange(rows, dtype=jnp.float32) / (rows - 1)
    spread = jnp.exp(jax.random.uniform(key, (rows, 1), jnp.float32, 0.0, math.log(4.0)))
    return base * ramp[:, None] * spread * lift


def base_values(key, rows, cols):
    first = jax.random.fold_in(key, 0)
    return jnp.clip(jax.random.normal(first, (rows, cols), jnp.float32), -4.0, 4.0)


def draw_tokens(key, part):
    key = jax.random.fold_in(key, 11)
    first, second = jax.random.split(key)
    values = rising_rows(second, base_values(first, TOKENS, D), 0.25)
    return values.astype(jnp.bfloat16)


def draw_cotangent(key, part):
    key = jax.random.fold_in(key, 23)
    first, second = jax.random.split(key)
    values = rising_rows(second, base_values(first, TOKENS, KV_WIDTH), 0.5)
    return values.astype(jnp.bfloat16)


def block_levels(own_key, extent, cuts, smallest, largest):
    factor_of = 1.0
    for dim, parts in cuts:
        heights = jax.random.uniform(jax.random.fold_in(jax.random.fold_in(own_key, 6), dim), (parts,), jnp.float32, smallest / len(cuts), largest / len(cuts))
        factor_of = factor_of * jnp.repeat(jnp.exp(heights), extent[dim] // parts).reshape((-1,) + (1,) * (len(extent) - 1 - dim))
    return factor_of


def centred(stream_key, shape, scale, reach, pieces=(), kind=jnp.bfloat16):
    factor_of = block_levels(stream_key, shape, pieces, -0.22, 0.18) if pieces else 1.0
    entries = jax.random.normal(stream_key, shape, jnp.float32) * scale * factor_of
    return jnp.minimum(jnp.maximum(entries, -reach), reach).astype(kind)


def setup_inputs(seed: int = 0) -> dict:
    splits = jax.random.split(jax.random.key(seed), 5)
    return {
        "tokens": draw_tokens(jax.random.fold_in(splits[4], 71), 0),
        "weight": centred(splits[1], (D, KV_WIDTH), D ** -0.5, 0.0625, ((0, 256),)),
        "cotangent": draw_cotangent(jax.random.fold_in(splits[4], 71), 0),
        "amax_history": jnp.clip(jax.random.uniform(splits[3], (3, HIST), jnp.float32, 0.5, 8.0), 0.5, 8.0),
    }


def reference(tokens, weight, cotangent, amax_history):
    keys = jnp.dot(tokens, weight, preferred_element_type=jnp.float32).astype(jnp.bfloat16)
    input_grad = lax.dot_general(cotangent, weight, (((1,), (1,)), ((), ())), preferred_element_type=jnp.float32).astype(jnp.bfloat16)
    summed = lax.dot_general(tokens, cotangent, (((0,), (0,)), ((), ())), preferred_element_type=jnp.float32)
    weight_grad = (summed * (1.0 / math.sqrt(TOKENS))).astype(jnp.bfloat16)
    amax = jnp.stack([jnp.max(jnp.abs(tokens.astype(jnp.float32))), jnp.max(jnp.abs(weight.astype(jnp.float32))), jnp.max(jnp.abs(cotangent.astype(jnp.float32)))])
    new_history = jnp.concatenate([amax[:, None], amax_history[:, :-1]], axis=1)
    return (keys, input_grad, weight_grad, new_history)
```

```python
import jax
import jax.numpy as jnp
from jax import lax
from jax.experimental import pallas as pl
from jax.experimental.pallas import tpu as pltpu
from jax.sharding import Mesh, PartitionSpec as P

AXES = ("z", "yh", "core", "x", "yl")
SIZES = (8, 2, 2, 4, 2)
PLANE = ("yh", "x", "yl")
ROWS = 256
KV = 512
HALF = 4096
CHUNK = 256
NOTE = 128
SENT = HALF + KV + NOTE
BOTH = 2 * ROWS
BF16, F32 = jnp.bfloat16, jnp.float32
VMEM_LIMIT = 48 * 1024 * 1024


def dot(a, b, contract):
    return lax.dot_general(a, b, ((contract[:1], contract[1:]), ((), ())), preferred_element_type=F32)


def top(a):
    a = jnp.abs(a)
    while a.shape[0] > 16:
        half = a.shape[0] // 2
        a = jnp.maximum(a[:half], a[half:])
    return jnp.max(jnp.max(a.astype(F32), axis=1, keepdims=True), axis=0, keepdims=True)


def normalise(m):
    x, k, s = m * 2.0**-24, jnp.full_like(m, -24.0), jnp.full_like(m, 2.0**-24)
    for b in (64, 32, 16, 8, 4, 2, 1):
        low = x < 2.0**-b
        x, k, s = jnp.where(low, x * 2.0**b, x), jnp.where(low, k + b, k), jnp.where(low, s * 2.0**b, s)
    return s, k


def bound_of(token_max, grad_max):
    return token_max * grad_max * float(BOTH)


def encode8(x):
    x2 = x * x
    x4 = x2 * x2
    return (x4 * x2) * (jnp.abs(x) * x)


def encode16(x):
    x2 = x * x
    x4 = x2 * x2
    x8 = x4 * x4
    return (x8 * x4) * (x2 * jnp.abs(x) * x)


def decode(y, power, shift):
    a = jnp.abs(y)
    v = jnp.where(a > 0.0, jnp.exp2(jnp.log2(a) * (1.0 / power) - shift), 0.0)
    return jnp.where(y < 0.0, -v, v)


def note(values, shape):
    rows = lax.broadcasted_iota(jnp.int32, shape, len(shape) - 2)
    out = jnp.zeros(shape, F32)
    for i, v in enumerate(values):
        out = jnp.where(rows == i, v, out)
    return out.astype(BF16)


def pack_kernel(core, tokens, cot, weight, sent, best):
    i = pl.program_id(0)
    other = pl.multiple_of((1 - core[0]) * CHUNK, CHUNK)
    width = tokens.shape[1] // (2 * CHUNK)
    for j in range(width):
        at = pl.multiple_of(i * (width * CHUNK) + j * CHUNK, CHUNK)
        sent[:, pl.ds(at, CHUNK)] = tokens[:, pl.ds(2 * CHUNK * j + other, CHUNK)]
    m = top(tokens[...])

    @pl.when(i == 0)
    def _():
        best[...] = jnp.zeros_like(best)

    best[...] = jnp.maximum(best[...], m)

    @pl.when(i == pl.num_programs(0) - 1)
    def _():
        sent[:, HALF:HALF + KV] = cot[...]
        sent[:, HALF + KV:] = note([best[:1, :1], top(weight[...]), top(cot[...])], (ROWS, NOTE))


def pack(core, tokens, cot, weight):
    steps = 4
    return pl.pallas_call(
        pack_kernel,
        out_shape=jax.ShapeDtypeStruct((ROWS, SENT), BF16),
        grid_spec=pltpu.PrefetchScalarGridSpec(
            num_scalar_prefetch=1,
            grid=(steps,),
            in_specs=[
                pl.BlockSpec((ROWS, 2 * HALF // steps), lambda i, c: (0, i)),
                pl.BlockSpec((ROWS, KV), lambda i, c: (0, 0)),
                pl.BlockSpec((32, KV), lambda i, c: (0, 0)),
            ],
            out_specs=pl.BlockSpec((ROWS, SENT), lambda i, c: (0, 0)),
            scratch_shapes=[pltpu.VMEM((8, 128), F32)],
        ),
        compiler_params=pltpu.CompilerParams(vmem_limit_bytes=VMEM_LIMIT),
        cost_estimate=pl.CostEstimate(flops=8_000_000, bytes_accessed=7_000_000, transcendentals=0),
        name="pack",
    )(core, tokens, cot, weight)


def grad_kernel(core, tokens, cot, own_note, got, got_cot, got_note, out):
    i = pl.program_id(0)
    own = pl.multiple_of(core[0] * CHUNK, CHUNK)
    notes = jnp.maximum(own_note[...].astype(F32), got_note[...].astype(F32))
    maxima = [notes[r:r + 1, 0:1] for r in range(3)]
    scale, k = normalise(maxima[0] * maxima[2] * float(2 * ROWS))
    scale = scale * 2.0**15
    pieces = got.shape[1] // CHUNK
    for j in range(pieces):
        mine = tokens[:, pl.ds(2 * CHUNK * j + own, CHUNK)]
        p = dot(mine, cot[...], (0, 0)) + dot(got[:, CHUNK * j:CHUNK * (j + 1)], got_cot[...], (0, 0))
        y = encode8(p * scale).astype(BF16)
        at = (i * (pieces // 2) + j // 2) * 2 * KV
        for d in range(8):
            for h in range(2):
                row = d * 32 + h * 16
                out[(j % 2) * 8 + d, :, pl.ds(pl.multiple_of(at + h * KV, KV), KV)] = y[row:row + 16, :]

    @pl.when(i == 0)
    def _():
        out[:, :, 2 * HALF:] = note(maxima + [k], (16, 16, NOTE))


def grad(core, tokens, cot, sent, got):
    steps = 4
    return pl.pallas_call(
        grad_kernel,
        out_shape=jax.ShapeDtypeStruct((16, 16, 2 * HALF + NOTE), BF16),
        grid_spec=pltpu.PrefetchScalarGridSpec(
            num_scalar_prefetch=1,
            grid=(steps,),
            in_specs=[
                pl.BlockSpec((ROWS, 2 * HALF // steps), lambda i, c: (0, i)),
                pl.BlockSpec((ROWS, KV), lambda i, c: (0, 0)),
                pl.BlockSpec((16, NOTE), lambda i, c: (0, (HALF + KV) // NOTE)),
                pl.BlockSpec((ROWS, HALF // steps), lambda i, c: (0, i)),
                pl.BlockSpec((ROWS, KV), lambda i, c: (0, HALF // KV)),
                pl.BlockSpec((16, NOTE), lambda i, c: (0, (HALF + KV) // NOTE)),
            ],
            out_specs=pl.BlockSpec((16, 16, 2 * HALF + NOTE), lambda i, c: (0, 0, 0)),
        ),
        compiler_params=pltpu.CompilerParams(vmem_limit_bytes=VMEM_LIMIT),
        cost_estimate=pl.CostEstimate(flops=2_200_000_000, bytes_accessed=11_000_000, transcendentals=0),
        name="grad",
    )(core, tokens, cot, sent, got, got, got)


def plane_kernel(parts, notes, out):
    maxima = [jnp.max(notes[:, r, :].astype(F32), axis=0, keepdims=True)[:, 0:1] for r in range(3)]
    width = 2 * KV
    for j in range(parts.shape[2] // width):
        total = jnp.zeros((16, width), F32)
        for s in range(16):
            shift = notes[s, 3:4, 0:1].astype(F32) + 15.0
            total += decode(parts[s, :, j * width:(j + 1) * width].astype(F32), 8, shift)
        scale, k = normalise(top(total))
        out[j, :, :width] = encode16(total * (scale * 2.0**7)).astype(BF16)
        out[j, :, width:] = note(maxima + [k], (16, NOTE))


def plane(parts):
    steps = 4
    return pl.pallas_call(
        plane_kernel,
        out_shape=jax.ShapeDtypeStruct((8, 16, 2 * KV + NOTE), BF16),
        grid=(steps,),
        in_specs=[
            pl.BlockSpec((16, 16, 2 * HALF // steps), lambda i: (0, 0, i)),
            pl.BlockSpec((16, 16, NOTE), lambda i: (0, 0, 2 * HALF // NOTE)),
        ],
        out_specs=pl.BlockSpec((8 // steps, 16, 2 * KV + NOTE), lambda i: (i, 0, 0)),
        compiler_params=pltpu.CompilerParams(vmem_limit_bytes=VMEM_LIMIT),
        cost_estimate=pl.CostEstimate(flops=20_000_000, bytes_accessed=5_000_000, transcendentals=4_000_000),
        name="plane",
    )(parts, parts)


def last_kernel(parts, history, weight_grad, new_history):
    total = jnp.zeros((16, 2 * KV), F32)
    for s in range(8):
        shift = parts[s, 3:4, 2 * KV:2 * KV + 1].astype(F32) + 7.0
        total += decode(parts[s, :, :2 * KV].astype(F32), 16, shift)
    total = (total * (1.0 / 256.0)).astype(BF16)
    weight_grad[:16, :] = total[:, :KV]
    weight_grad[16:, :] = total[:, KV:]
    notes = jnp.max(parts[:, :, 2 * KV:].astype(F32), axis=0)
    new_history[...] = jnp.concatenate([notes[:3, :1], history[:, :15]], axis=1)


def last(parts, history):
    return pl.pallas_call(
        last_kernel,
        out_shape=(jax.ShapeDtypeStruct((32, KV), BF16), jax.ShapeDtypeStruct((3, 16), F32)),
        compiler_params=pltpu.CompilerParams(vmem_limit_bytes=VMEM_LIMIT),
        cost_estimate=pl.CostEstimate(flops=1_000_000, bytes_accessed=330_000, transcendentals=260_000),
        name="last",
    )(parts, history)


def theirs_kernel(tokens, cot, weight, input_grad, keys):
    i = pl.program_id(0)
    w = weight[...]
    p = dot(tokens[...], w, (1, 0))

    @pl.when(i == 0)
    def _():
        keys[...] = p

    @pl.when(i > 0)
    def _():
        keys[...] += p

    input_grad[...] = dot(cot[...], w, (1, 1)).astype(BF16)


def theirs(got, weight):
    steps = 4
    return pl.pallas_call(
        theirs_kernel,
        out_shape=(jax.ShapeDtypeStruct((ROWS, HALF), BF16), jax.ShapeDtypeStruct((ROWS, KV), F32)),
        grid=(steps,),
        in_specs=[
            pl.BlockSpec((ROWS, HALF // steps), lambda i: (0, i)),
            pl.BlockSpec((ROWS, KV), lambda i: (0, HALF // KV)),
            pl.BlockSpec((HALF // steps, KV), lambda i: (i, 0)),
        ],
        out_specs=(
            pl.BlockSpec((ROWS, HALF // steps), lambda i: (0, i)),
            pl.BlockSpec((ROWS, KV), lambda i: (0, 0)),
        ),
        compiler_params=pltpu.CompilerParams(vmem_limit_bytes=VMEM_LIMIT),
        cost_estimate=pl.CostEstimate(flops=2_200_000_000, bytes_accessed=9_000_000, transcendentals=0),
        name="theirs",
    )(got, got, weight)


def ours_kernel(core, tokens, cot, weight, input_grad, keys):
    i = pl.program_id(0)
    own = pl.multiple_of(core[0] * CHUNK, CHUNK)
    total = jnp.zeros((ROWS, KV), F32)
    for j in range(weight.shape[0] // CHUNK):
        w = weight[j * CHUNK:(j + 1) * CHUNK, :]
        total += dot(tokens[:, pl.ds(2 * CHUNK * j + own, CHUNK)], w, (1, 0))
        input_grad[:, pl.ds(2 * CHUNK * j + own, CHUNK)] = dot(cot[...], w, (1, 1)).astype(BF16)

    @pl.when(i == 0)
    def _():
        keys[...] = total

    @pl.when(i > 0)
    def _():
        keys[...] += total


def ours(core, tokens, cot, weight):
    steps = 4
    return pl.pallas_call(
        ours_kernel,
        out_shape=(jax.ShapeDtypeStruct((ROWS, 2 * HALF), BF16), jax.ShapeDtypeStruct((ROWS, KV), F32)),
        grid_spec=pltpu.PrefetchScalarGridSpec(
            num_scalar_prefetch=1,
            grid=(steps,),
            in_specs=[
                pl.BlockSpec((ROWS, 2 * HALF // steps), lambda i, c: (0, i)),
                pl.BlockSpec((ROWS, KV), lambda i, c: (0, 0)),
                pl.BlockSpec((HALF // steps, KV), lambda i, c: (i, 0)),
            ],
            out_specs=(
                pl.BlockSpec((ROWS, 2 * HALF // steps), lambda i, c: (0, i)),
                pl.BlockSpec((ROWS, KV), lambda i, c: (0, 0)),
            ),
        ),
        compiler_params=pltpu.CompilerParams(vmem_limit_bytes=VMEM_LIMIT),
        cost_estimate=pl.CostEstimate(flops=2_200_000_000, bytes_accessed=12_000_000, transcendentals=0),
        name="ours",
    )(core, tokens, cot, weight)


def join_kernel(core, columns, ours_keys, got_keys, _, input_grad, keys, sem):
    other = pl.multiple_of((1 - core[0]) * CHUNK, CHUNK)
    copies = [
        pltpu.make_async_copy(
            columns.at[:, pl.ds(j * CHUNK, CHUNK)],
            input_grad.at[:, pl.ds(2 * CHUNK * j + other, CHUNK)],
            sem.at[j],
        )
        for j in range(HALF // CHUNK)
    ]
    for c in copies:
        c.start()
    keys[...] = (ours_keys[...] + got_keys[...]).astype(BF16)
    for c in copies:
        c.wait()


def join(core, columns, ours_keys, got_keys, input_grad):
    return pl.pallas_call(
        join_kernel,
        out_shape=(jax.ShapeDtypeStruct((ROWS, 2 * HALF), BF16), jax.ShapeDtypeStruct((ROWS, KV), BF16)),
        in_specs=[
            pl.BlockSpec(memory_space=pltpu.SMEM),
            pl.BlockSpec(memory_space=pl.ANY),
            pl.BlockSpec(memory_space=pltpu.VMEM),
            pl.BlockSpec(memory_space=pltpu.VMEM),
            pl.BlockSpec(memory_space=pl.ANY),
        ],
        out_specs=(pl.BlockSpec(memory_space=pl.ANY), pl.BlockSpec(memory_space=pltpu.VMEM)),
        scratch_shapes=[pltpu.SemaphoreType.DMA((HALF // CHUNK,))],
        input_output_aliases={4: 0},
        compiler_params=pltpu.CompilerParams(vmem_limit_bytes=VMEM_LIMIT),
        cost_estimate=pl.CostEstimate(flops=130_000, bytes_accessed=5_400_000, transcendentals=0),
        name="join",
    )(core, columns, ours_keys, got_keys, input_grad)


SWAP = [(0, 1), (1, 0)]


def local(tokens, weight, cot, history):
    core = lax.axis_index("core").astype(jnp.int32).reshape(1)
    sent = pack(core, tokens, cot, weight)
    got = lax.ppermute(sent, "core", SWAP)
    near = lax.all_to_all(jnp.broadcast_to(weight[None], (16, 32, KV)), PLANE, 0, 0, tiled=True)
    half_weight = lax.all_gather(near.reshape(512, KV), "z", axis=0, tiled=True)
    coded = grad(core, tokens, cot, sent, got)
    parts = lax.all_to_all(coded, PLANE, 0, 0, tiled=True)
    parts = lax.all_to_all(plane(parts), "z", 0, 0, tiled=True)
    weight_grad, new_history = last(parts, history)
    columns, their_keys = theirs(got, half_weight)
    columns = lax.ppermute(columns, "core", SWAP)
    got_keys = lax.ppermute(their_keys, "core", SWAP)
    input_grad, our_keys = ours(core, tokens, cot, half_weight)
    input_grad, keys = join(core, columns, our_keys, got_keys, input_grad)
    return (keys, input_grad, weight_grad, new_history)


def solution(mesh):
    split = Mesh(mesh.devices.reshape(SIZES), AXES)
    rows = P(AXES, None)
    return jax.shard_map(
        local,
        mesh=split,
        in_specs=(rows, rows, rows, P()),
        out_specs=(rows, rows, rows, P()),
        check_vma=False,
    )
```
